32 devices in a mesh: expert: 8 (over z, x), tensor: 4 (over y, core).
Axes of the slice: x: 2, y: 2, z: 4, core: 2. Of those that a mesh axis runs over, the one named last changes fastest.
Arguments:
- attn_vals: bfloat16 [512, 4096], P('expert', 'tensor'), may hold values from -6 to 6
- residual: bfloat16 [512, 4096], P('expert', 'tensor'), may hold values from -6 to 6
- out_weight: bfloat16 [4096, 4096], P('tensor'), may hold values from -0.09375 to 0.09375
- norm_gain: float32 [4096], P('tensor'), may hold values from 0.5 to 1.5
- router_weight: float32 [4096, 8], P('tensor'), may hold values from -0.09375 to 0.09375
- routes: int32 [512, 2], P('expert'), may hold values from 0 to 7, all different within a row; in each aligned block of 64 rows (0 to 63, 64 to 127, ...) at most 32 rows name the same one
- w_gate: bfloat16 [8, 4096, 8192], P('expert', None, 'tensor'), may hold values from -0.09375 to 0.09375
- w_up: bfloat16 [8, 4096, 8192], P('expert', None, 'tensor'), may hold values from -0.09375 to 0.09375
- w_down: bfloat16 [8, 8192, 4096], P('expert', 'tensor'), may hold values from -0.0625 to 0.0625
- slab_of: int32 [8], replicated, may hold values from 0 to 7, each once
- final_gain: float32 [4096], P('tensor'), may hold values from 0.5 to 1.5
- row_order: int32 [512], replicated, may hold values from 0 to 511, each once
Outputs:
- stream_out: bfloat16 [512, 4096], P('expert', 'tensor')
- normed_out: bfloat16 [512, 4096], P('expert', 'tensor')
The draws below stay inside these ranges and needn't reach their ends.
Inputs may be any that keep to these rules, and one draw needn't show every extreme that they name: `routes`: the two experts of a row differ. In each aligned block of 64 rows (the rows of one device) no expert is named by more than 32 rows, and some block names one expert exactly 32 times. `slab_of`: A permutation. `row_order`: A permutation.
All inputs are finite; a program needn't handle non-finite values.
Results may differ from the reference program's by a relative error of at most 0.017.
Values may be sent and summed in bfloat16 or wider, within the bound.
A program may use at most 128 MiB of HBM per device.

```python
import math
import jax
import jax.numpy as jnp
import numpy as np
from jax import lax

D = 4096
FF = 8192
EXPERTS = 8
ROWS_DEV = 64
MOST = 32
ROWS = 512
FFS = 8192
N_EXPERT = 8
N_TENSOR = 4


def steps_of(rng, extent, cuts, least, high):
    def one(position, shards_of):
        heights = jax.random.uniform(jax.random.fold_in(jax.random.fold_in(rng, 6), position), (shards_of,), jnp.float32, least / len(cuts), high / len(cuts))
        return jnp.repeat(jnp.exp(heights), extent[position] // shards_of).reshape((-1,) + (1,) * (len(extent) - position - 1))

    gain = one(*cuts[0])
    for cut in cuts[1:]:
        gain = gain * one(*cut)
    return gain


def routed_block(rng, own, number, rows, count, top, bound, skew):
    sequence = jax.random.permutation(rng, count)
    crowded, usual = shares(count, rows * top, bound, skew, True), shares(count, rows * top, bound, skew, False)
    places = jnp.arange(count)

    def named(tallies, turn):
        used = int((tallies > 0).sum())
        fixed = max(1, used // 4)
        passed = fixed + (places - fixed + turn * (used - fixed)) % max(1, count - fixed)
        return jnp.zeros((count,), jnp.int32).at[sequence[jnp.where(places < fixed, places, passed)]].set(jnp.asarray(tallies, jnp.int32))

    tallies = jnp.where(number % 4 == 0, named(crowded, number // 4), named(usual, number - number // 4 - 1))
    mixed = jax.random.permutation(jax.random.fold_in(own, 3), count)
    giver, receiver = mixed[0:count // 2 * 2:2], mixed[1:count // 2 * 2:2]
    margin = jnp.minimum(tallies[giver] - 1, bound - tallies[receiver]) // 2
    margin = jnp.where((giver == sequence[0]) | (receiver == sequence[0]) | (tallies[receiver] == 0), 0, jnp.maximum(margin, 0))
    passed = jax.random.randint(jax.random.fold_in(own, 4), (count // 2,), 0, 1 << 20) % (margin + 1)
    tallies = tallies.at[giver].add(-passed).at[receiver].add(passed)
    items = jnp.searchsorted(jnp.cumsum(tallies), jnp.arange(rows * top), side="right").astype(jnp.int32)
    grid = items.reshape(top, rows).T
    grid = grid[jax.random.permutation(jax.random.fold_in(own, 1), rows)]
    turn = jax.random.randint(jax.random.fold_in(own, 2), (rows, 1), 0, top)
    return jnp.take_along_axis(grid, (jnp.arange(top)[None, :] + turn) % top, axis=1)


def shares(count, total, most, slope, full):
    loads = [(1 << 20) // math.isqrt(grade ** slope) + 1 for grade in range(1, count + 1)]
    largest = most if full else min(most, max(-(-total // count), total * loads[0] // sum(loads)))
    least = 1 if total - largest >= count - 1 else 0
    counts, spare = [largest] + [least] * (count - 1), total - largest - least * (count - 1)
    while spare > 0:
        free = [i for i in range(1, count) if counts[i] < largest] or [i for i in range(1, count) if counts[i] < most]
        pool, left = sum([loads[i] for i in free]), spare
        for i in free:
            addition = min(most - counts[i], max(1, left * loads[i] // pool), spare)
            counts[i] = counts[i] + addition
            spare = spare - addition
    return np.array(counts)


def scatter_about(stream_key, shape, deviation, most, cuts=(), kind=jnp.bfloat16):
    entries = jax.random.normal(stream_key, shape, jnp.float32) * deviation
    if len(cuts) > 0:
        entries = steps_of(stream_key, shape, cuts, -0.22, 0.18) * entries
    return jnp.clip(entries, min=-most, max=most).astype(kind)


def setup_inputs(seed: int = 0) -> dict:
    splits = jax.random.split(jax.random.key(seed), 13)
    attn_vals = scatter_about(splits[0], (ROWS, D), 1.0, 6.0, ((0, 8), (1, 4)))
    residual = scatter_about(splits[1], (ROWS, D), 1.0, 6.0, ((0, 8), (1, 4)))
    out_weight = scatter_about(splits[2], (D, D), D ** -0.5, 0.09375, ((0, 4),))
    norm_gain = jnp.clip(1.0 + 0.1 * jax.random.normal(splits[3], (D,), jnp.float32), 0.5, 1.5)
    router_weight = scatter_about(splits[4], (D, EXPERTS), D ** -0.5, 0.09375, ((0, 4),), jnp.float32)
    routes_keys = jax.random.split(jax.random.fold_in(splits[5], 1), ROWS // ROWS_DEV)
    routes_turns = jax.random.permutation(jax.random.fold_in(splits[5], 3), ROWS // ROWS_DEV)
    routes = jax.vmap(lambda own, number: routed_block(jax.random.fold_in(splits[5], 2), own, number, ROWS_DEV, EXPERTS, 2, MOST, 2))(routes_keys, routes_turns).reshape((ROWS, 2))
    w_gate = scatter_about(splits[6], (N_EXPERT, D, FFS), D ** -0.5, 0.09375, ((0, 8), (2, 4)))
    w_up = scatter_about(splits[7], (N_EXPERT, D, FFS), D ** -0.5, 0.09375, ((0, 8), (2, 4)))
    w_down = scatter_about(splits[8], (N_EXPERT, FFS, D), FF ** -0.5, 0.0625, ((0, 8), (1, 4)))
    slab_of = jax.random.permutation(splits[9], N_EXPERT).astype(jnp.int32)
    final_gain = jnp.clip(1.0 + 0.1 * jax.random.normal(splits[10], (D,), jnp.float32), 0.5, 1.5)
    row_order = jax.random.permutation(splits[11], ROWS).astype(jnp.int32)
    return {"attn_vals": attn_vals, "residual": residual, "out_weight": out_weight, "norm_gain": norm_gain, "router_weight": router_weight, "routes": routes, "w_gate": w_gate, "w_up": w_up, "w_down": w_down, "slab_of": slab_of, "final_gain": final_gain, "row_order": row_order}


EPS = 1e-05

def reference(attn_vals, residual, out_weight, norm_gain, router_weight, routes, w_gate, w_up, w_down, slab_of, final_gain, row_order):
    project = jnp.dot(attn_vals, out_weight, preferred_element_type=jnp.float32)
    stream_in = (residual.astype(jnp.float32) + project).astype(jnp.bfloat16)
    hidden_f = stream_in.astype(jnp.float32)
    scaled = hidden_f * norm_gain
    inverse_rms = lax.rsqrt(lax.optimization_barrier(jnp.mean(hidden_f * hidden_f, axis=1)) + EPS)
    normed_in = (scaled * inverse_rms[:, None]).astype(jnp.bfloat16)
    logits = jnp.dot(scaled, router_weight, precision=lax.Precision.HIGHEST) * inverse_rms[:, None]
    chosen = jnp.take_along_axis(logits, routes, axis=1)
    leading = jax.nn.sigmoid(chosen[:, 0] - chosen[:, 1])
    mixing = jnp.stack([leading, 1.0 - leading], axis=1)
    slab_count = N_EXPERT // EXPERTS
    per_block = FF // (slab_count * N_TENSOR)
    holders = jnp.zeros((N_EXPERT,), jnp.int32).at[slab_of].set(jnp.arange(N_EXPERT, dtype=jnp.int32))
    holders = holders.reshape(EXPERTS, slab_count)
    capacity = N_EXPERT * MOST

    def one_expert(totals, expert):
        picked = routes == expert
        member = jnp.any(picked, axis=1)
        index_list = jnp.nonzero(member, size=capacity, fill_value=0)[0].astype(jnp.int32)
        valid = (jnp.arange(capacity) < jnp.sum(member.astype(jnp.int32))).astype(jnp.float32)
        inputs = normed_in[index_list].astype(jnp.float32)
        owner = holders[expert]
        gate_val = jnp.einsum('cd,sdf->csf', inputs, w_gate[owner].astype(jnp.float32))
        up_val = jnp.einsum('cd,sdf->csf', inputs, w_up[owner].astype(jnp.float32))
        active = (jax.nn.silu(gate_val) * up_val).astype(jnp.bfloat16)
        active = active.reshape(capacity, slab_count, N_TENSOR, per_block).astype(jnp.float32)
        down_w = w_down[owner].reshape(slab_count, N_TENSOR, per_block, D).astype(jnp.float32)
        pieces = jnp.einsum('cstf,stfd->cstd', active, down_w).astype(jnp.bfloat16)
        pieces = lax.optimization_barrier(pieces)
        slab_sum = lax.optimization_barrier(jnp.sum(pieces.astype(jnp.float32), axis=2)).astype(jnp.bfloat16)
        slab_sum = lax.optimization_barrier(slab_sum)
        output = lax.optimization_barrier(jnp.sum(slab_sum.astype(jnp.float32), axis=1))
        factor = lax.optimization_barrier(jnp.sum(jnp.where(picked[index_list], mixing[index_list], 0.0), axis=1)) * valid
        return (totals.at[index_list].add(output * factor[:, None]), None)
    blended, _ = lax.scan(one_expert, jnp.zeros((ROWS, D), jnp.float32), jnp.arange(EXPERTS, dtype=jnp.int32))
    stream = (hidden_f + blended).astype(jnp.bfloat16)
    stream_f = stream.astype(jnp.float32)
    final_rms = lax.rsqrt(lax.optimization_barrier(jnp.mean(stream_f * stream_f, axis=1)) + EPS)
    normed = (stream_f * final_rms[:, None] * final_gain).astype(jnp.bfloat16)
    source = jnp.zeros((ROWS,), jnp.int32).at[row_order].set(jnp.arange(ROWS, dtype=jnp.int32))
    return (stream[source], normed[source])
```

```python
import functools

import jax
import jax.numpy as jnp
from jax import lax
from jax.experimental import pallas as pl
from jax.experimental.pallas import tpu as pltpu
from jax.sharding import PartitionSpec as P

MOST = 32
EPS = 1e-05
BF = jnp.bfloat16
F32 = jnp.float32


def dot(a, b):
    return jnp.dot(a, b, preferred_element_type=F32)


def layer_kernel(
    groups,
    parts,
    attn,
    residual,
    out_w,
    gain,
    router,
    routes,
    w_gate,
    w_up,
    w_down,
    slots,
    final_gain,
    order,
    stream_out,
    normed_out,
    ow,
    wg,
    wu,
    wd,
    proj_send,
    proj_recv,
    stat_send,
    stat_recv,
    out_rows,
    arr,
    act,
    part,
    sib,
    cross_send,
    cross_recv,
    slab,
    ret,
    all_stream,
    sq_send,
    sq_recv,
    w_sem,
    send_sem,
    recv_sem,
):
    e = lax.axis_index("expert")
    t = lax.axis_index("tensor")
    ny = parts // 2
    y, c = t // 2, t % 2
    rows, dl = residual.shape
    d_model = dl * parts
    count = router.shape[1]
    fl = act.shape[1]
    half = fl // 2
    slots_all = groups * MOST

    def part_of(yo, co, sign):
        core = c if co == 0 else 1 - c
        return lax.rem(y + sign * yo + ny, ny) * 2 + core

    used = [0]

    def remote(src, dst, dev):
        k = used[0]
        used[0] += 1
        return pltpu.make_async_remote_copy(
            src_ref=src,
            dst_ref=dst,
            send_sem=send_sem.at[k],
            recv_sem=recv_sem.at[k],
            device_id=dev,
            device_id_type=pl.DeviceIdType.MESH,
        )

    def at_part(j, sign=1):
        return (e, part_of(j // 2, j % 2, sign))

    def at_group(o, sign=1):
        return (lax.rem(e + sign * o + groups, groups), t)

    ow_copies = []
    for n, j in enumerate(list(range(1, parts)) + [0]):
        col = pl.multiple_of(part_of(j // 2, j % 2, 1) * dl, dl)
        cp = pltpu.make_async_copy(out_w.at[:, pl.ds(col, dl)], ow.at[j], w_sem.at[n])
        cp.start()
        ow_copies.append(cp)

    barrier = pltpu.get_barrier_semaphore()
    for j in range(1, parts):
        pl.semaphore_signal(barrier, inc=1, device_id=at_part(j), device_id_type=pl.DeviceIdType.MESH)
    for o in range(1, groups):
        pl.semaphore_signal(barrier, inc=1, device_id=at_group(o), device_id_type=pl.DeviceIdType.MESH)
    pl.semaphore_wait(barrier, parts + groups - 2)

    proj_copies = []
    own = None
    for n, j in enumerate(list(range(1, parts)) + [0]):
        ow_copies[n].wait()
        value = dot(attn[...], ow[j])
        if j:
            proj_send[j - 1] = value.astype(BF)
            cp = remote(proj_send.at[j - 1], proj_recv.at[j - 1], at_part(j))
            cp.start()
            proj_copies.append(cp)
        else:
            own = value.astype(BF).astype(F32)

    gu_copies, wd_copies = [], []
    n = parts
    for j in range(parts):
        row = pl.multiple_of(part_of(j // 2, j % 2, -1) * dl, dl)
        for src, dst in ((w_gate, wg), (w_up, wu)):
            cp = pltpu.make_async_copy(src.at[0, pl.ds(row, dl), :], dst.at[j], w_sem.at[n])
            cp.start()
            gu_copies.append(cp)
            n += 1
    for j in range(parts):
        col = pl.multiple_of(part_of(j // 2, j % 2, 1) * dl, dl)
        for k, dst in ((0, wd.at[j]), (1, ow.at[j, pl.ds(0, half), :])):
            cp = pltpu.make_async_copy(
                w_down.at[0, pl.ds(k * half, half), pl.ds(col, dl)], dst, w_sem.at[n]
            )
            cp.start()
            wd_copies.append(cp)
            n += 1

    route_f = routes[...].astype(F32)
    ids = lax.broadcasted_iota(jnp.int32, (rows, count), 1).astype(F32)
    hot = [jnp.where(route_f[:, k : k + 1] == ids, 1.0, 0.0) for k in range(2)]
    ri = lax.broadcasted_iota(jnp.int32, (rows, rows), 0)
    ci = lax.broadcasted_iota(jnp.int32, (rows, rows), 1)
    lower = jnp.where(ci < ri, 1.0, 0.0).astype(BF)
    before = dot(lower, (hot[0] + hot[1]).astype(BF))
    sel = []
    for k in range(2):
        place = jnp.sum(hot[k] * before, axis=1, keepdims=True)
        hit = jnp.where(slots[0:1, :] == route_f[:, k : k + 1], 1.0, 0.0)
        fit = jnp.where(slots[1:2, :] == place, 1.0, 0.0)
        sel.append(hit * fit)
    placing = (sel[0] + sel[1]).astype(BF)
    sel = [s.astype(BF) for s in sel]

    for cp in proj_copies:
        cp.wait_recv()
    for j in range(parts - 1):
        own = own + proj_recv[j].astype(F32)
    own = own.astype(BF).astype(F32)
    hidden = (residual[...].astype(F32) + own).astype(BF).astype(F32)
    scaled = hidden * gain[...]
    stat_send[...] = jnp.zeros_like(stat_send)
    stat_send[:, 0:count] = jnp.dot(
        scaled, router[...], precision=lax.Precision.HIGHEST, preferred_element_type=F32
    )
    stat_send[:, count : count + 1] = jnp.sum(hidden * hidden, axis=1, keepdims=True)
    stat_copies = []
    for j in range(1, parts):
        cp = remote(stat_send, stat_recv.at[j - 1], at_part(j))
        cp.start()
        stat_copies.append(cp)
    stats = stat_send[...]
    for cp in stat_copies:
        cp.wait_recv()
    for j in range(parts - 1):
        stats = stats + stat_recv[j]
    inverse = lax.rsqrt(stats[:, count : count + 1] / d_model + EPS)
    normed_in = (scaled * inverse).astype(BF)
    logits = stats[:, 0:count] * inverse
    chosen = [jnp.sum(hot[k] * logits, axis=1, keepdims=True) for k in range(2)]
    first = 1.0 / (1.0 + jnp.exp(chosen[1] - chosen[0]))
    mixing = [first, 1.0 - first]

    out_rows[...] = lax.dot_general(
        placing, normed_in, (((0,), (0,)), ((), ())), preferred_element_type=F32
    ).astype(BF)
    out_copies = []
    for o in range(1, groups):
        part_rows = pl.ds(o * MOST, MOST)
        cp = remote(out_rows.at[part_rows], arr.at[0, part_rows], at_group(o))
        cp.start()
        out_copies.append(cp)
    arr[0, 0:MOST] = out_rows[0:MOST]
    for cp in out_copies:
        cp.wait_recv()

    spread = [remote(arr.at[0], arr.at[2 * yo], at_part(2 * yo)) for yo in range(1, ny)]
    spread_sib = remote(arr.at[0], arr.at[1], at_part(1))
    for cp in spread:
        cp.start()
    spread_sib.start()
    passed = []
    for yo in range(1, ny):
        spread[yo - 1].wait_recv()
        cp = remote(arr.at[2 * yo], arr.at[2 * yo + 1], at_part(1))
        cp.start()
        passed.append(cp)
    spread_sib.wait_recv()
    for cp in passed:
        cp.wait_recv()
    for cp in gu_copies:
        cp.wait()

    rc = min(256, slots_all)
    fc = min(256, fl)

    @pl.loop(0, slots_all // rc)
    def _(r):
        rr = pl.ds(pl.multiple_of(r * rc, rc), rc)

        @pl.loop(0, fl // fc)
        def _(f):
            cc = pl.ds(pl.multiple_of(f * fc, fc), fc)
            gate = dot(arr[0, rr, :], wg[0, :, cc])
            up = dot(arr[0, rr, :], wu[0, :, cc])
            for j in range(1, parts):
                gate += dot(arr[j, rr, :], wg[j, :, cc])
                up += dot(arr[j, rr, :], wu[j, :, cc])
            act[rr, cc] = (gate / (1.0 + jnp.exp(-gate)) * up).astype(BF)

    for cp in wd_copies:
        cp.wait()
    dc = min(256, dl)

    def down(j):
        @pl.loop(0, slots_all // rc)
        def _(r):
            rr = pl.ds(pl.multiple_of(r * rc, rc), rc)

            @pl.loop(0, dl // dc)
            def _(f):
                cc = pl.ds(pl.multiple_of(f * dc, dc), dc)
                value = dot(act[rr, 0:half], wd[j, :, cc])
                value += dot(act[rr, half:fl], ow[j, 0:half, cc])
                part[j, rr, cc] = value.astype(BF)

    sib_copies = []
    yos = list(range(1, ny)) + [0]
    for yo in yos:
        down(2 * yo + 1)
        cp = remote(part.at[2 * yo + 1], sib.at[yo], at_part(1))
        cp.start()
        sib_copies.append(cp)
    cross = []
    for n, yo in enumerate(yos):
        down(2 * yo)
        sib_copies[n].wait_recv()
        if yo:
            cross_send[yo - 1] = (part[2 * yo].astype(F32) + sib[yo].astype(F32)).astype(BF)
            cp = remote(cross_send.at[yo - 1], cross_recv.at[yo - 1], at_part(2 * yo))
            cp.start()
            cross.append(cp)
    for cp in cross:
        cp.wait_recv()
    total = part[0].astype(F32) + sib[0].astype(F32)
    for yo in range(1, ny):
        total = total + cross_recv[yo - 1].astype(F32)
    slab[...] = total.astype(BF)

    back = []
    for o in range(1, groups):
        part_rows = pl.ds(o * MOST, MOST)
        cp = remote(slab.at[part_rows], ret.at[part_rows], at_group(o, -1))
        cp.start()
        back.append(cp)
    ret[0:MOST] = slab[0:MOST]
    for cp in back:
        cp.wait_recv()
    blended = mixing[0] * dot(sel[0], ret[...]) + mixing[1] * dot(sel[1], ret[...])
    all_stream[0:rows] = (hidden + blended).astype(BF)

    moved = []
    for o in range(1, groups):
        cp = remote(
            all_stream.at[pl.ds(0, rows)], all_stream.at[pl.ds(o * rows, rows)], at_group(o)
        )
        cp.start()
        moved.append(cp)
    want = lax.broadcasted_iota(jnp.int32, (rows, groups * rows), 0).astype(F32)
    pick = jnp.where(order[...] == want, 1.0, 0.0).astype(BF)
    for cp in moved:
        cp.wait_recv()
    stream = dot(pick, all_stream[...])
    stream_out[...] = stream.astype(BF)
    sq_send[...] = jnp.broadcast_to(jnp.sum(stream * stream, axis=1, keepdims=True), sq_send.shape)
    sq_copies = []
    for j in range(1, parts):
        cp = remote(sq_send, sq_recv.at[j - 1], at_part(j))
        cp.start()
        sq_copies.append(cp)
    square = sq_send[...]
    for cp in sq_copies:
        cp.wait_recv()
    for j in range(parts - 1):
        square = square + sq_recv[j]
    factor = lax.rsqrt(square[:, 0:1] / d_model + EPS)
    normed_out[...] = (stream * factor * final_gain[...]).astype(BF)

    started = proj_copies + stat_copies + out_copies + spread + [spread_sib] + passed
    for cp in started + sib_copies + cross + back + moved + sq_copies:
        cp.wait_send()


def on_device(
    attn_vals,
    residual,
    out_weight,
    norm_gain,
    router_weight,
    routes,
    w_gate,
    w_up,
    w_down,
    slab_of,
    final_gain,
    row_order,
):
    groups = lax.axis_size("expert")
    parts = lax.axis_size("tensor")
    ny = parts // 2
    e = lax.axis_index("expert")
    rows, dl = residual.shape
    d_model = out_weight.shape[1]
    slab_count = groups // router_weight.shape[1]
    fl = w_gate.shape[2]
    slots_all = groups * MOST
    steps = jnp.arange(groups, dtype=jnp.int32)
    held = jnp.take(slab_of // slab_count, (e + steps) % groups)
    slots = jnp.stack(
        [jnp.repeat(held, MOST), jnp.arange(slots_all, dtype=jnp.int32) % MOST]
    ).astype(F32)
    order = jnp.take(row_order.reshape(groups, rows), (e - steps) % groups, axis=0)
    order = (order.reshape(1, groups * rows) - e * rows).astype(F32)
    vmem = pl.BlockSpec(memory_space=pltpu.VMEM)
    hbm = pl.BlockSpec(memory_space=pl.ANY)
    copies = 3 * (parts - 1) + 3 * (groups - 1) + 2 * (ny - 1) + 1 + ny + ny - 1
    flops = 2 * (rows * dl * d_model + 3 * slots_all * d_model * fl)
    moved = 2 * (dl * d_model + 3 * d_model * fl)
    call = pl.pallas_call(
        functools.partial(layer_kernel, groups, parts),
        out_shape=[jax.ShapeDtypeStruct((rows, dl), BF)] * 2,
        in_specs=[vmem, vmem, hbm, vmem, vmem, vmem, hbm, hbm, hbm, vmem, vmem, vmem],
        out_specs=[vmem, vmem],
        scratch_shapes=[
            pltpu.VMEM((parts, dl, dl), BF),
            pltpu.VMEM((parts, dl, fl), BF),
            pltpu.VMEM((parts, dl, fl), BF),
            pltpu.VMEM((parts, fl // 2, dl), BF),
            pltpu.VMEM((parts - 1, rows, dl), BF),
            pltpu.VMEM((parts - 1, rows, dl), BF),
            pltpu.VMEM((rows, 128), F32),
            pltpu.VMEM((parts - 1, rows, 128), F32),
            pltpu.VMEM((slots_all, dl), BF),
            pltpu.VMEM((parts, slots_all, dl), BF),
            pltpu.VMEM((slots_all, fl), BF),
            pltpu.VMEM((parts, slots_all, dl), BF),
            pltpu.VMEM((ny, slots_all, dl), BF),
            pltpu.VMEM((max(ny - 1, 1), slots_all, dl), BF),
            pltpu.VMEM((max(ny - 1, 1), slots_all, dl), BF),
            pltpu.VMEM((slots_all, dl), BF),
            pltpu.VMEM((slots_all, dl), BF),
            pltpu.VMEM((groups * rows, dl), BF),
            pltpu.VMEM((rows, 128), F32),
            pltpu.VMEM((parts - 1, rows, 128), F32),
            pltpu.SemaphoreType.DMA((5 * parts,)),
            pltpu.SemaphoreType.DMA((copies,)),
            pltpu.SemaphoreType.DMA((copies,)),
        ],
        compiler_params=pltpu.CompilerParams(
            collective_id=0, has_side_effects=True, vmem_limit_bytes=62 * 2**20
        ),
        cost_estimate=pl.CostEstimate(flops=flops, bytes_accessed=moved, transcendentals=0),
    )
    return call(
        attn_vals,
        residual,
        out_weight,
        norm_gain.reshape(1, dl),
        router_weight,
        routes,
        w_gate,
        w_up,
        w_down,
        slots,
        final_gain.reshape(1, dl),
        order,
    )


def solution(mesh):
    return jax.shard_map(
        on_device,
        mesh=mesh,
        in_specs=(
            P("expert", "tensor"),
            P("expert", "tensor"),
            P("tensor", None),
            P("tensor"),
            P("tensor", None),
            P("expert", None),
            P("expert", None, "tensor"),
            P("expert", None, "tensor"),
            P("expert", "tensor", None),
            P(),
            P("tensor"),
            P(),
        ),
        out_specs=(P("expert", "tensor"), P("expert", "tensor")),
        check_vma=False,
    )
```

```python
import functools

import jax
import jax.numpy as jnp
from jax import lax
from jax.experimental import pallas as pl
from jax.experimental.pallas import tpu as pltpu
from jax.sharding import PartitionSpec as P

MOST = 32
EPS = 1e-05
BF = jnp.bfloat16
F32 = jnp.float32


def dot(a, b):
    return jnp.dot(a, b, preferred_element_type=F32)


def layer_kernel(
    groups,
    parts,
    attn,
    residual,
    out_w,
    gain,
    router,
    routes,
    w_gate,
    w_up,
    w_down,
    slab_of,
    order,
    stream_out,
    factor_out,
    ow,
    wg,
    wu,
    wd,
    proj_send,
    proj_recv,
    stat_send,
    stat_recv,
    out_rows,
    arr,
    act,
    part,
    sib,
    cross_send,
    cross_recv,
    slab,
    ret,
    all_stream,
    sq_send,
    sq_recv,
    w_sem,
    send_sem,
    recv_sem,
):
    e = lax.axis_index("expert")
    t = lax.axis_index("tensor")
    ny = parts // 2
    y, c = t // 2, t % 2
    rows, dl = residual.shape
    d_model = dl * parts
    count = router.shape[0]
    slab_count = groups // count
    chunks, _, wide = slab.shape
    fl = act.shape[1]
    half = fl // 2
    slots_all = groups * MOST

    def part_of(yo, co, sign):
        core = c if co == 0 else 1 - c
        return lax.rem(y + sign * yo + ny, ny) * 2 + core

    used = [0]

    def remote(src, dst, dev):
        k = used[0]
        used[0] += 1
        return pltpu.make_async_remote_copy(
            src_ref=src,
            dst_ref=dst,
            send_sem=send_sem.at[k],
            recv_sem=recv_sem.at[k],
            device_id=dev,
            device_id_type=pl.DeviceIdType.MESH,
        )

    def at_part(j, sign=1):
        return (e, part_of(j // 2, j % 2, sign))

    def at_group(o, sign=1):
        return (lax.rem(e + sign * o + groups, groups), t)

    ow_copies = []
    for n, j in enumerate(list(range(1, parts)) + [0]):
        col = pl.multiple_of(part_of(j // 2, j % 2, 1) * dl, dl)
        cp = pltpu.make_async_copy(out_w.at[:, pl.ds(col, dl)], ow.at[j], w_sem.at[n])
        cp.start()
        ow_copies.append(cp)

    barrier = pltpu.get_barrier_semaphore()
    for j in range(1, parts):
        pl.semaphore_signal(barrier, inc=1, device_id=at_part(j), device_id_type=pl.DeviceIdType.MESH)
    for o in range(1, groups):
        pl.semaphore_signal(barrier, inc=1, device_id=at_group(o), device_id_type=pl.DeviceIdType.MESH)
    pl.semaphore_wait(barrier, parts + groups - 2)

    proj_copies = []
    own = None
    for n, j in enumerate(list(range(1, parts)) + [0]):
        ow_copies[n].wait()
        value = dot(attn[...], ow[j])
        if j:
            proj_send[j - 1] = value.astype(BF)
            cp = remote(proj_send.at[j - 1], proj_recv.at[j - 1], at_part(j))
            cp.start()
            proj_copies.append(cp)
        else:
            own = value.astype(BF).astype(F32)

    gu_copies, wd_copies = [], []
    n = parts
    for j in range(parts):
        row = pl.multiple_of(part_of(j // 2, j % 2, -1) * dl, dl)
        for src, dst in ((w_gate, wg), (w_up, wu)):
            cp = pltpu.make_async_copy(src.at[0, pl.ds(row, dl), :], dst.at[j], w_sem.at[n])
            cp.start()
            gu_copies.append(cp)
            n += 1
    for j in range(parts):
        col = pl.multiple_of(part_of(j // 2, j % 2, 1) * dl, dl)
        for k, dst in ((0, wd.at[j]), (1, ow.at[j, pl.ds(0, half), :])):
            cp = pltpu.make_async_copy(
                w_down.at[0, pl.ds(k * half, half), pl.ds(col, dl)], dst, w_sem.at[n]
            )
            cp.start()
            wd_copies.append(cp)
            n += 1

    ri = lax.broadcasted_iota(jnp.int32, (rows, rows), 0)
    ci = lax.broadcasted_iota(jnp.int32, (rows, rows), 1)
    same = jnp.where(ci == ri, 1.0, 0.0).astype(BF)
    route_f = lax.dot_general(
        same,
        routes[...].astype(F32).astype(BF),
        (((1,), (1,)), ((), ())),
        preferred_element_type=F32,
    )
    column = lax.broadcasted_iota(jnp.int32, (1, slots_all), 1)
    held = jnp.zeros((1, slots_all), F32)
    slot = column
    for o in range(groups):
        expert = lax.div(slab_of[lax.rem(e + o, groups)], slab_count).astype(F32)
        held = jnp.where(column >= o * MOST, expert, held)
        slot = jnp.where(column >= o * MOST, column - o * MOST, slot)
    slot = slot.astype(F32)
    ids = lax.broadcasted_iota(jnp.int32, (rows, count), 1).astype(F32)
    hot = [jnp.where(route_f[:, k : k + 1] == ids, 1.0, 0.0) for k in range(2)]
    lower = jnp.where(ci < ri, 1.0, 0.0).astype(BF)
    before = dot(lower, (hot[0] + hot[1]).astype(BF))
    sel = []
    for k in range(2):
        place = jnp.sum(hot[k] * before, axis=1, keepdims=True)
        hit = jnp.where(held == route_f[:, k : k + 1], 1.0, 0.0)
        fit = jnp.where(slot == place, 1.0, 0.0)
        sel.append(hit * fit)
    placing = (sel[0] + sel[1]).astype(BF)
    sel = [s.astype(BF) for s in sel]

    for cp in proj_copies:
        cp.wait_recv()
    for j in range(parts - 1):
        own = own + proj_recv[j].astype(F32)
    own = own.astype(BF).astype(F32)
    hidden = (residual[...].astype(F32) + own).astype(BF).astype(F32)
    scaled = hidden * gain[...]
    stat_send[...] = jnp.zeros_like(stat_send)
    stat_send[:, 0:count] = lax.dot_general(
        scaled,
        router[...],
        (((1,), (1,)), ((), ())),
        precision=lax.Precision.HIGHEST,
        preferred_element_type=F32,
    )
    stat_send[:, count : count + 1] = jnp.sum(hidden * hidden, axis=1, keepdims=True)
    stat_copies = []
    for j in range(1, parts):
        cp = remote(stat_send, stat_recv.at[j - 1], at_part(j))
        cp.start()
        stat_copies.append(cp)
    stats = stat_send[...]
    for cp in stat_copies:
        cp.wait_recv()
    for j in range(parts - 1):
        stats = stats + stat_recv[j]
    inverse = lax.rsqrt(stats[:, count : count + 1] / d_model + EPS)
    normed_in = (scaled * inverse).astype(BF)
    logits = stats[:, 0:count] * inverse
    chosen = [jnp.sum(hot[k] * logits, axis=1, keepdims=True) for k in range(2)]
    first = 1.0 / (1.0 + jnp.exp(chosen[1] - chosen[0]))
    mixing = [first, 1.0 - first]

    out_rows[...] = lax.dot_general(
        placing, normed_in, (((0,), (0,)), ((), ())), preferred_element_type=F32
    ).astype(BF)
    out_copies = []
    for o in range(1, groups):
        part_rows = pl.ds(o * MOST, MOST)
        cp = remote(out_rows.at[part_rows], arr.at[0, part_rows], at_group(o))
        cp.start()
        out_copies.append(cp)
    arr[0, 0:MOST] = out_rows[0:MOST]
    pieces = 4 if groups % 4 == 0 else 1
    per = groups // pieces
    spread, waiting = [], []

    def forward():
        for cp in waiting.pop(0):
            cp[0].wait_recv()
            cp[1].start()
            spread.append(cp[1])

    last = []
    for q in range(pieces):
        for o in range(max(q * per, 1), (q + 1) * per):
            out_copies[o - 1].wait_recv()
        block = pl.ds(q * per * MOST, per * MOST)
        pairs = []
        for yo in range(1, ny):
            cp = remote(arr.at[0, block], arr.at[2 * yo, block], at_part(2 * yo))
            cp.start()
            spread.append(cp)
            on = remote(arr.at[2 * yo, block], arr.at[2 * yo + 1, block], at_part(1))
            pairs.append((cp, on))
            last.append(on)
        cp = remote(arr.at[0, block], arr.at[1, block], at_part(1))
        cp.start()
        spread.append(cp)
        last.append(cp)
        waiting.append(pairs)
        if q:
            forward()
    forward()
    for cp in last:
        cp.wait_recv()
    for cp in gu_copies:
        cp.wait()

    rc = min(256, slots_all)
    fc = min(256, fl)

    @pl.loop(0, slots_all // rc)
    def _(r):
        rr = pl.ds(pl.multiple_of(r * rc, rc), rc)

        @pl.loop(0, fl // fc)
        def _(f):
            cc = pl.ds(pl.multiple_of(f * fc, fc), fc)
            gate = dot(arr[0, rr, :], wg[0, :, cc])
            up = dot(arr[0, rr, :], wu[0, :, cc])
            for j in range(1, parts):
                gate += dot(arr[j, rr, :], wg[j, :, cc])
                up += dot(arr[j, rr, :], wu[j, :, cc])
            act[rr, cc] = (gate / (1.0 + jnp.exp(-gate)) * up).astype(BF)

    for cp in wd_copies:
        cp.wait()
    dc = min(256, wide)

    def down(j, f):
        @pl.loop(0, slots_all // rc)
        def _(r):
            rr = pl.ds(pl.multiple_of(r * rc, rc), rc)

            @pl.loop(0, wide // dc)
            def _(n):
                to = pl.ds(pl.multiple_of(n * dc, dc), dc)
                cc = pl.ds(pl.multiple_of(f * wide + n * dc, dc), dc)
                value = dot(act[rr, 0:half], wd[j, :, cc])
                value += dot(act[rr, half:fl], ow[j, 0:half, cc])
                part[f, j, rr, to] = value.astype(BF)

    sib_copies, cross, back, moved = [], [], [], []
    yos = list(range(1, ny)) + [0]
    crossing = []
    for f in range(chunks):
        mine = []
        for yo in yos:
            down(2 * yo + 1, f)
            cp = remote(part.at[f, 2 * yo + 1], sib.at[f, yo], at_part(1))
            cp.start()
            mine.append(cp)
        sib_copies += mine
        row = []
        for n, yo in enumerate(yos):
            down(2 * yo, f)
            mine[n].wait_recv()
            if yo:
                cross_send[f, yo - 1] = (
                    part[f, 2 * yo].astype(F32) + sib[f, yo].astype(F32)
                ).astype(BF)
                cp = remote(cross_send.at[f, yo - 1], cross_recv.at[f, yo - 1], at_part(2 * yo))
                cp.start()
                row.append(cp)
        crossing.append(row)
        cross += row

    returning = []
    for f in range(chunks):
        total = part[f, 0].astype(F32) + sib[f, 0].astype(F32)
        for yo in range(1, ny):
            crossing[f][yo - 1].wait_recv()
            total = total + cross_recv[f, yo - 1].astype(F32)
        slab[f] = total.astype(BF)
        row = []
        for o in range(1, groups):
            block = pl.ds(o * MOST, MOST)
            cp = remote(slab.at[f, block], ret.at[f, block], at_group(o, -1))
            cp.start()
            row.append(cp)
        ret[f, 0:MOST] = slab[f, 0:MOST]
        returning.append(row)
        back += row

    side = lax.rem(e, 2)
    pair = e // 2
    pairs_all = groups // 2
    partner = (e + 1 - 2 * side, t)

    def block_of(device):
        return pl.ds(pl.multiple_of(device * rows, rows), rows)

    first_hop, second_hop = [], []
    for f in range(chunks):
        for cp in returning[f]:
            cp.wait_recv()
        blended = mixing[0] * dot(sel[0], ret[f]) + mixing[1] * dot(sel[1], ret[f])
        own_rows = block_of(e)
        all_stream[f, own_rows] = (hidden[:, f * wide : (f + 1) * wide] + blended).astype(BF)
        row = []
        for o in range(1, pairs_all):
            to = lax.rem(pair + o, pairs_all) * 2 + side
            cp = remote(all_stream.at[f, own_rows], all_stream.at[f, own_rows], (to, t))
            cp.start()
            row.append(cp)
        cp = remote(all_stream.at[f, own_rows], all_stream.at[f, own_rows], partner)
        cp.start()
        second_hop.append(cp)
        first_hop.append(row)
        moved += row + [cp]
    for f in range(chunks):
        for o in range(1, pairs_all):
            first_hop[f][o - 1].wait_recv()
            source = block_of(lax.rem(pair - o + pairs_all, pairs_all) * 2 + side)
            cp = remote(all_stream.at[f, source], all_stream.at[f, source], partner)
            cp.start()
            second_hop.append(cp)
            moved.append(cp)
    want = lax.broadcasted_iota(jnp.int32, (rows, groups * rows), 0)
    pick = jnp.where(order[...] - e * rows == want, 1.0, 0.0).astype(BF)
    for cp in second_hop:
        cp.wait_recv()
    squares = jnp.zeros((rows, 1), F32)
    for f in range(chunks):
        stream = dot(pick, all_stream[f])
        stream_out[:, f * wide : (f + 1) * wide] = stream
        squares = squares + jnp.sum(stream * stream, axis=1, keepdims=True)
    sq_send[...] = jnp.broadcast_to(squares, sq_send.shape)
    sq_copies = []
    for j in range(1, parts):
        cp = remote(sq_send, sq_recv.at[j - 1], at_part(j))
        cp.start()
        sq_copies.append(cp)
    square = sq_send[...]
    for cp in sq_copies:
        cp.wait_recv()
    for j in range(parts - 1):
        square = square + sq_recv[j]
    factor_out[...] = lax.rsqrt(square / d_model + EPS)

    started = proj_copies + stat_copies + out_copies + spread
    for cp in started + sib_copies + cross + back + moved + sq_copies:
        cp.wait_send()


def on_device(
    attn_vals,
    residual,
    out_weight,
    norm_gain,
    router_weight,
    routes,
    w_gate,
    w_up,
    w_down,
    slab_of,
    final_gain,
    row_order,
):
    groups = lax.axis_size("expert")
    parts = lax.axis_size("tensor")
    ny = parts // 2
    rows, dl = residual.shape
    d_model = out_weight.shape[1]
    fl = w_gate.shape[2]
    slots_all = groups * MOST
    wide = 512 if dl % 512 == 0 else dl
    chunks = dl // wide
    pieces = 4 if groups % 4 == 0 else 1
    vmem = pl.BlockSpec(memory_space=pltpu.VMEM)
    hbm = pl.BlockSpec(memory_space=pl.ANY)
    smem = pl.BlockSpec(memory_space=pltpu.SMEM)
    copies = 3 * (parts - 1) + groups - 1 + pieces * (2 * ny - 1)
    copies += chunks * (2 * ny - 1 + 2 * (groups - 1))
    flops = 2 * (rows * dl * d_model + 3 * slots_all * d_model * fl)
    moved = 2 * (dl * d_model + 3 * d_model * fl)
    call = pl.pallas_call(
        functools.partial(layer_kernel, groups, parts),
        out_shape=[
            jax.ShapeDtypeStruct((rows, dl), F32),
            jax.ShapeDtypeStruct((rows, 128), F32),
        ],
        in_specs=[vmem, vmem, hbm, vmem, vmem, vmem, hbm, hbm, hbm, smem, vmem],
        out_specs=[vmem, vmem],
        scratch_shapes=[
            pltpu.VMEM((parts, dl, dl), BF),
            pltpu.VMEM((parts, dl, fl), BF),
            pltpu.VMEM((parts, dl, fl), BF),
            pltpu.VMEM((parts, fl // 2, dl), BF),
            pltpu.VMEM((parts - 1, rows, dl), BF),
            pltpu.VMEM((parts - 1, rows, dl), BF),
            pltpu.VMEM((rows, 128), F32),
            pltpu.VMEM((parts - 1, rows, 128), F32),
            pltpu.VMEM((slots_all, dl), BF),
            pltpu.VMEM((parts, slots_all, dl), BF),
            pltpu.VMEM((slots_all, fl), BF),
            pltpu.VMEM((chunks, parts, slots_all, wide), BF),
            pltpu.VMEM((chunks, ny, slots_all, wide), BF),
            pltpu.VMEM((chunks, max(ny - 1, 1), slots_all, wide), BF),
            pltpu.VMEM((chunks, max(ny - 1, 1), slots_all, wide), BF),
            pltpu.VMEM((chunks, slots_all, wide), BF),
            pltpu.VMEM((chunks, slots_all, wide), BF),
            pltpu.VMEM((chunks, groups * rows, wide), BF),
            pltpu.VMEM((rows, 128), F32),
            pltpu.VMEM((parts - 1, rows, 128), F32),
            pltpu.SemaphoreType.DMA((5 * parts,)),
            pltpu.SemaphoreType.DMA((copies,)),
            pltpu.SemaphoreType.DMA((copies,)),
        ],
        compiler_params=pltpu.CompilerParams(
            collective_id=0, has_side_effects=True, vmem_limit_bytes=62 * 2**20
        ),
        cost_estimate=pl.CostEstimate(flops=flops, bytes_accessed=moved, transcendentals=0),
    )
    stream, factor = call(
        attn_vals,
        residual,
        out_weight,
        norm_gain.reshape(1, dl),
        router_weight.T,
        routes.T,
        w_gate,
        w_up,
        w_down,
        slab_of,
        row_order.reshape(1, groups * rows),
    )
    normed = stream * factor[:, 0:1] * final_gain[None, :]
    return stream.astype(BF), normed.astype(BF)


def solution(mesh):
    return jax.shard_map(
        on_device,
        mesh=mesh,
        in_specs=(
            P("expert", "tensor"),
            P("expert", "tensor"),
            P("tensor", None),
            P("tensor"),
            P("tensor", None),
            P("expert", None),
            P("expert", None, "tensor"),
            P("expert", None, "tensor"),
            P("expert", "tensor", None),
            P(),
            P("tensor"),
            P(),
        ),
        out_specs=(P("expert", "tensor"), P("expert", "tensor")),
        check_vma=False,
    )
```

```python
import functools

import jax
import jax.numpy as jnp
from jax import lax
from jax.experimental import pallas as pl
from jax.experimental.pallas import tpu as pltpu
from jax.sharding import PartitionSpec as P

MOST = 32
EPS = 1e-05
BF = jnp.bfloat16
F32 = jnp.float32


def dot(a, b):
    return jnp.dot(a, b, preferred_element_type=F32)


def layer_kernel(
    groups,
    parts,
    attn,
    residual,
    out_w,
    gain,
    router,
    routes,
    w_gate,
    w_up,
    w_down,
    slab_of,
    order,
    final_gain,
    stream_out,
    normed_out,
    ow,
    wg,
    wu,
    wd,
    proj_send,
    proj_recv,
    stat_send,
    stat_recv,
    out_rows,
    arr,
    act,
    part,
    sib,
    cross_send,
    cross_recv,
    slab,
    ret,
    all_stream,
    sq_send,
    sq_recv,
    w_sem,
    send_sem,
    recv_sem,
):
    e = lax.axis_index("expert")
    t = lax.axis_index("tensor")
    ny = parts // 2
    y, c = t // 2, t % 2
    rows, dl = residual.shape
    d_model = dl * parts
    count = router.shape[0]
    slab_count = groups // count
    chunks, _, wide = slab.shape
    fl = act.shape[1]
    half = fl // 2
    slots_all = groups * MOST

    def part_of(yo, co, sign):
        core = c if co == 0 else 1 - c
        return lax.rem(y + sign * yo + ny, ny) * 2 + core

    used = [0]

    def remote(src, dst, dev):
        k = used[0]
        used[0] += 1
        return pltpu.make_async_remote_copy(
            src_ref=src,
            dst_ref=dst,
            send_sem=send_sem.at[k],
            recv_sem=recv_sem.at[k],
            device_id=dev,
            device_id_type=pl.DeviceIdType.MESH,
        )

    def at_part(j, sign=1):
        return (e, part_of(j // 2, j % 2, sign))

    def at_group(o, sign=1):
        return (lax.rem(e + sign * o + groups, groups), t)

    ow_copies = []
    for n, j in enumerate(list(range(1, parts)) + [0]):
        col = pl.multiple_of(part_of(j // 2, j % 2, 1) * dl, dl)
        cp = pltpu.make_async_copy(out_w.at[:, pl.ds(col, dl)], ow.at[j], w_sem.at[n])
        cp.start()
        ow_copies.append(cp)

    barrier = pltpu.get_barrier_semaphore()
    for j in range(1, parts):
        pl.semaphore_signal(barrier, inc=1, device_id=at_part(j), device_id_type=pl.DeviceIdType.MESH)
    for o in range(1, groups):
        pl.semaphore_signal(barrier, inc=1, device_id=at_group(o), device_id_type=pl.DeviceIdType.MESH)
    pl.semaphore_wait(barrier, parts + groups - 2)

    proj_copies = []
    own = None
    for n, j in enumerate(list(range(1, parts)) + [0]):
        ow_copies[n].wait()
        value = dot(attn[...], ow[j])
        if j:
            proj_send[j - 1] = value.astype(BF)
            cp = remote(proj_send.at[j - 1], proj_recv.at[j - 1], at_part(j))
            cp.start()
            proj_copies.append(cp)
        else:
            own = value.astype(BF).astype(F32)

    gu_copies, wd_copies = [], []
    n = parts
    for j in range(parts):
        row = pl.multiple_of(part_of(j // 2, j % 2, -1) * dl, dl)
        for src, dst in ((w_gate, wg), (w_up, wu)):
            cp = pltpu.make_async_copy(src.at[0, pl.ds(row, dl), :], dst.at[j], w_sem.at[n])
            cp.start()
            gu_copies.append(cp)
            n += 1
    for j in range(parts):
        col = pl.multiple_of(part_of(j // 2, j % 2, 1) * dl, dl)
        for k, dst in ((0, wd.at[j]), (1, ow.at[j, pl.ds(0, half), :])):
            cp = pltpu.make_async_copy(
                w_down.at[0, pl.ds(k * half, half), pl.ds(col, dl)], dst, w_sem.at[n]
            )
            cp.start()
            wd_copies.append(cp)
            n += 1

    ri = lax.broadcasted_iota(jnp.int32, (rows, rows), 0)
    ci = lax.broadcasted_iota(jnp.int32, (rows, rows), 1)
    same = jnp.where(ci == ri, 1.0, 0.0).astype(BF)
    route_f = lax.dot_general(
        same,
        routes[...].astype(F32).astype(BF),
        (((1,), (1,)), ((), ())),
        preferred_element_type=F32,
    )
    column = lax.broadcasted_iota(jnp.int32, (1, slots_all), 1)
    held = jnp.zeros((1, slots_all), F32)
    slot = column
    for o in range(groups):
        expert = lax.div(slab_of[lax.rem(e + o, groups)], slab_count).astype(F32)
        held = jnp.where(column >= o * MOST, expert, held)
        slot = jnp.where(column >= o * MOST, column - o * MOST, slot)
    slot = slot.astype(F32)
    ids = lax.broadcasted_iota(jnp.int32, (rows, count), 1).astype(F32)
    hot = [jnp.where(route_f[:, k : k + 1] == ids, 1.0, 0.0) for k in range(2)]
    lower = jnp.where(ci < ri, 1.0, 0.0).astype(BF)
    before = dot(lower, (hot[0] + hot[1]).astype(BF))
    sel = []
    for k in range(2):
        place = jnp.sum(hot[k] * before, axis=1, keepdims=True)
        hit = jnp.where(held == route_f[:, k : k + 1], 1.0, 0.0)
        fit = jnp.where(slot == place, 1.0, 0.0)
        sel.append(hit * fit)
    placing = (sel[0] + sel[1]).astype(BF)
    sel = [s.astype(BF) for s in sel]

    for cp in proj_copies:
        cp.wait_recv()
    for j in range(parts - 1):
        own = own + proj_recv[j].astype(F32)
    own = own.astype(BF).astype(F32)
    hidden = (residual[...].astype(F32) + own).astype(BF).astype(F32)
    scaled = hidden * gain[...]
    stat_send[...] = jnp.zeros_like(stat_send)
    stat_send[:, 0:count] = lax.dot_general(
        scaled,
        router[...],
        (((1,), (1,)), ((), ())),
        precision=lax.Precision.HIGHEST,
        preferred_element_type=F32,
    )
    stat_send[:, count : count + 1] = jnp.sum(hidden * hidden, axis=1, keepdims=True)
    stat_copies = []
    for j in range(1, parts):
        cp = remote(stat_send, stat_recv.at[j - 1], at_part(j))
        cp.start()
        stat_copies.append(cp)
    stats = stat_send[...]
    for cp in stat_copies:
        cp.wait_recv()
    for j in range(parts - 1):
        stats = stats + stat_recv[j]
    inverse = lax.rsqrt(stats[:, count : count + 1] / d_model + EPS)
    normed_in = (scaled * inverse).astype(BF)
    logits = stats[:, 0:count] * inverse
    chosen = [jnp.sum(hot[k] * logits, axis=1, keepdims=True) for k in range(2)]
    first = 1.0 / (1.0 + jnp.exp(chosen[1] - chosen[0]))
    mixing = [first, 1.0 - first]

    out_rows[...] = lax.dot_general(
        placing, normed_in, (((0,), (0,)), ((), ())), preferred_element_type=F32
    ).astype(BF)
    out_copies = []
    for o in range(1, groups):
        part_rows = pl.ds(o * MOST, MOST)
        cp = remote(out_rows.at[part_rows], arr.at[0, part_rows], at_group(o))
        cp.start()
        out_copies.append(cp)
    arr[0, 0:MOST] = out_rows[0:MOST]
    pieces = 4 if groups % 4 == 0 else 1
    per = groups // pieces
    spread, waiting = [], []

    def forward():
        for cp in waiting.pop(0):
            cp[0].wait_recv()
            cp[1].start()
            spread.append(cp[1])

    last = []
    for q in range(pieces):
        for o in range(max(q * per, 1), (q + 1) * per):
            out_copies[o - 1].wait_recv()
        block = pl.ds(q * per * MOST, per * MOST)
        pairs = []
        for yo in range(1, ny):
            cp = remote(arr.at[0, block], arr.at[2 * yo, block], at_part(2 * yo))
            cp.start()
            spread.append(cp)
            on = remote(arr.at[2 * yo, block], arr.at[2 * yo + 1, block], at_part(1))
            pairs.append((cp, on))
            last.append(on)
        cp = remote(arr.at[0, block], arr.at[1, block], at_part(1))
        cp.start()
        spread.append(cp)
        last.append(cp)
        waiting.append(pairs)
        if q:
            forward()
    forward()
    for cp in last:
        cp.wait_recv()
    for cp in gu_copies:
        cp.wait()

    rc = min(256, slots_all)
    fc = min(256, fl)

    @pl.loop(0, slots_all // rc)
    def _(r):
        rr = pl.ds(pl.multiple_of(r * rc, rc), rc)

        @pl.loop(0, fl // fc)
        def _(f):
            cc = pl.ds(pl.multiple_of(f * fc, fc), fc)
            gate = dot(arr[0, rr, :], wg[0, :, cc])
            up = dot(arr[0, rr, :], wu[0, :, cc])
            for j in range(1, parts):
                gate += dot(arr[j, rr, :], wg[j, :, cc])
                up += dot(arr[j, rr, :], wu[j, :, cc])
            act[rr, cc] = (gate / (1.0 + jnp.exp(-gate)) * up).astype(BF)

    for cp in wd_copies:
        cp.wait()
    dc = min(256, wide)

    def down(j, f):
        @pl.loop(0, slots_all // rc)
        def _(r):
            rr = pl.ds(pl.multiple_of(r * rc, rc), rc)

            @pl.loop(0, wide // dc)
            def _(n):
                to = pl.ds(pl.multiple_of(n * dc, dc), dc)
                cc = pl.ds(pl.multiple_of(f * wide + n * dc, dc), dc)
                value = dot(act[rr, 0:half], wd[j, :, cc])
                value += dot(act[rr, half:fl], ow[j, 0:half, cc])
                part[f, j, rr, to] = value.astype(BF)

    sib_copies, cross, back, moved = [], [], [], []
    yos = list(range(1, ny)) + [0]
    crossing = []
    for f in range(chunks):
        mine = []
        for yo in yos:
            down(2 * yo + 1, f)
            cp = remote(part.at[f, 2 * yo + 1], sib.at[f, yo], at_part(1))
            cp.start()
            mine.append(cp)
        sib_copies += mine
        row = []
        for n, yo in enumerate(yos):
            down(2 * yo, f)
            mine[n].wait_recv()
            if yo:
                cross_send[f, yo - 1] = (
                    part[f, 2 * yo].astype(F32) + sib[f, yo].astype(F32)
                ).astype(BF)
                cp = remote(cross_send.at[f, yo - 1], cross_recv.at[f, yo - 1], at_part(2 * yo))
                cp.start()
                row.append(cp)
        crossing.append(row)
        cross += row

    returning = []
    for f in range(chunks):
        total = part[f, 0].astype(F32) + sib[f, 0].astype(F32)
        for yo in range(1, ny):
            crossing[f][yo - 1].wait_recv()
            total = total + cross_recv[f, yo - 1].astype(F32)
        slab[f] = total.astype(BF)
        row = []
        for o in range(1, groups):
            block = pl.ds(o * MOST, MOST)
            cp = remote(slab.at[f, block], ret.at[f, block], at_group(o, -1))
            cp.start()
            row.append(cp)
        ret[f, 0:MOST] = slab[f, 0:MOST]
        returning.append(row)
        back += row

    side = lax.rem(e, 2)
    pair = e // 2
    pairs_all = groups // 2
    partner = (e + 1 - 2 * side, t)

    def block_of(device):
        return pl.ds(pl.multiple_of(device * rows, rows), rows)

    first_hop, second_hop = [], []
    for f in range(chunks):
        for cp in returning[f]:
            cp.wait_recv()
        blended = mixing[0] * dot(sel[0], ret[f]) + mixing[1] * dot(sel[1], ret[f])
        own_rows = block_of(e)
        all_stream[f, own_rows] = (hidden[:, f * wide : (f + 1) * wide] + blended).astype(BF)
        row = []
        for o in range(1, pairs_all):
            to = lax.rem(pair + o, pairs_all) * 2 + side
            cp = remote(all_stream.at[f, own_rows], all_stream.at[f, own_rows], (to, t))
            cp.start()
            row.append(cp)
        cp = remote(all_stream.at[f, own_rows], all_stream.at[f, own_rows], partner)
        cp.start()
        second_hop.append(cp)
        first_hop.append(row)
        moved += row + [cp]
    for f in range(chunks):
        for o in range(1, pairs_all):
            first_hop[f][o - 1].wait_recv()
            source = block_of(lax.rem(pair - o + pairs_all, pairs_all) * 2 + side)
            cp = remote(all_stream.at[f, source], all_stream.at[f, source], partner)
            cp.start()
            second_hop.append(cp)
            moved.append(cp)
    want = lax.broadcasted_iota(jnp.int32, (rows, groups * rows), 0)
    pick = jnp.where(order[...] - e * rows == want, 1.0, 0.0).astype(BF)
    for cp in second_hop:
        cp.wait_recv()
    squares = jnp.zeros((rows, 1), F32)
    for f in range(chunks):
        stream = dot(pick, all_stream[f])
        stream_out[:, f * wide : (f + 1) * wide] = stream
        squares = squares + jnp.sum(stream * stream, axis=1, keepdims=True)
    sq_send[...] = jnp.broadcast_to(squares, sq_send.shape)
    sq_copies = []
    for j in range(1, parts):
        cp = remote(sq_send, sq_recv.at[j - 1], at_part(j))
        cp.start()
        sq_copies.append(cp)
    square = sq_send[...]
    for cp in sq_copies:
        cp.wait_recv()
    for j in range(parts - 1):
        square = square + sq_recv[j]
    factor = lax.rsqrt(square[:, 0:1] / d_model + EPS)
    normed_out[...] = stream_out[...] * factor * final_gain[...]

    started = proj_copies + stat_copies + out_copies + spread
    for cp in started + sib_copies + cross + back + moved + sq_copies:
        cp.wait_send()


def on_device(
    attn_vals,
    residual,
    out_weight,
    norm_gain,
    router_weight,
    routes,
    w_gate,
    w_up,
    w_down,
    slab_of,
    final_gain,
    row_order,
):
    groups = lax.axis_size("expert")
    parts = lax.axis_size("tensor")
    ny = parts // 2
    rows, dl = residual.shape
    d_model = out_weight.shape[1]
    fl = w_gate.shape[2]
    slots_all = groups * MOST
    wide = 256 if dl % 256 == 0 else dl
    chunks = dl // wide
    pieces = 4 if groups % 4 == 0 else 1
    vmem = pl.BlockSpec(memory_space=pltpu.VMEM)
    hbm = pl.BlockSpec(memory_space=pl.ANY)
    smem = pl.BlockSpec(memory_space=pltpu.SMEM)
    copies = 3 * (parts - 1) + groups - 1 + pieces * (2 * ny - 1)
    copies += chunks * (2 * ny - 1 + 2 * (groups - 1))
    flops = 2 * (rows * dl * d_model + 3 * slots_all * d_model * fl)
    moved = 2 * (dl * d_model + 3 * d_model * fl)
    call = pl.pallas_call(
        functools.partial(layer_kernel, groups, parts),
        out_shape=[jax.ShapeDtypeStruct((rows, dl), F32)] * 2,
        in_specs=[vmem, vmem, hbm, vmem, vmem, vmem, hbm, hbm, hbm, smem, vmem, vmem],
        out_specs=[vmem, vmem],
        scratch_shapes=[
            pltpu.VMEM((parts, dl, dl), BF),
            pltpu.VMEM((parts, dl, fl), BF),
            pltpu.VMEM((parts, dl, fl), BF),
            pltpu.VMEM((parts, fl // 2, dl), BF),
            pltpu.VMEM((parts - 1, rows, dl), BF),
            pltpu.VMEM((parts - 1, rows, dl), BF),
            pltpu.VMEM((rows, 128), F32),
            pltpu.VMEM((parts - 1, rows, 128), F32),
            pltpu.VMEM((slots_all, dl), BF),
            pltpu.VMEM((parts, slots_all, dl), BF),
            pltpu.VMEM((slots_all, fl), BF),
            pltpu.VMEM((chunks, parts, slots_all, wide), BF),
            pltpu.VMEM((chunks, ny, slots_all, wide), BF),
            pltpu.VMEM((chunks, max(ny - 1, 1), slots_all, wide), BF),
            pltpu.VMEM((chunks, max(ny - 1, 1), slots_all, wide), BF),
            pltpu.VMEM((chunks, slots_all, wide), BF),
            pltpu.VMEM((chunks, slots_all, wide), BF),
            pltpu.VMEM((chunks, groups * rows, wide), BF),
            pltpu.VMEM((rows, 128), F32),
            pltpu.VMEM((parts - 1, rows, 128), F32),
            pltpu.SemaphoreType.DMA((5 * parts,)),
            pltpu.SemaphoreType.DMA((copies,)),
            pltpu.SemaphoreType.DMA((copies,)),
        ],
        compiler_params=pltpu.CompilerParams(
            collective_id=0, has_side_effects=True, vmem_limit_bytes=62 * 2**20
        ),
        cost_estimate=pl.CostEstimate(flops=flops, bytes_accessed=moved, transcendentals=0),
    )
    stream, normed = call(
        attn_vals,
        residual,
        out_weight,
        norm_gain.reshape(1, dl),
        router_weight.T,
        routes.T,
        w_gate,
        w_up,
        w_down,
        slab_of,
        row_order.reshape(1, groups * rows),
        final_gain.reshape(1, dl),
    )
    return stream.astype(BF), normed.astype(BF)


def solution(mesh):
    return jax.shard_map(
        on_device,
        mesh=mesh,
        in_specs=(
            P("expert", "tensor"),
            P("expert", "tensor"),
            P("tensor", None),
            P("tensor"),
            P("tensor", None),
            P("expert", None),
            P("expert", None, "tensor"),
            P("expert", None, "tensor"),
            P("expert", "tensor", None),
            P(),
            P("tensor"),
            P(),
        ),
        out_specs=(P("expert", "tensor"), P("expert", "tensor")),
        check_vma=False,
    )
```
